512 devices in a mesh: row: 16 (over y, core), col: 32 (over x, z).
Axes of the slice: x: 4, y: 8, z: 8, core: 2. Of those that a mesh axis runs over, the one named last changes fastest.
Arguments:
- diag_inverse: bfloat16 [2048, 2048], P(None, 'col'), as said below
- row_v: bfloat16 [16, 2048, 512], P('row', 'col'), may hold values from -0.8984375 to 0.8984375
- row_rank: int32 [16], P('row'), may hold values from 64 to 512, as said below
- col_v: bfloat16 [64, 2048, 512], P('col', 'row'), may hold values from -0.8984375 to 0.8984375
- col_rank: int32 [64], P('col'), may hold values from 64 to 512, as said below
Outputs:
- solved_v: bfloat16 [16, 2048, 512], P('row', 'col')
- coupling: bfloat16 [16, 64, 512, 512], P('row', 'col')
The draws below stay inside these ranges and needn't reach their ends.
Inputs may be any that keep to these rules, and one draw needn't show every extreme that they name: `row_rank`: each rank is one of 64, 128, 256, 512; both the smallest and the largest occur. `col_rank`: each rank is one of 64, 128, 256, 512; both the smallest and the largest occur. `diag_inverse`: lower triangular with a diagonal between 0.5 and 2.
All inputs are finite; a program needn't handle non-finite values.
Results may differ from the reference program's by a relative error of at most 0.0055.
Values may be sent and summed in bfloat16 or wider, within the bound.
A program may use at most 64 MiB of HBM per device.

```python
import jax
import jax.numpy as jnp
from jax import lax

TILE = 2048
RANK_MAX = 512
ROW_TILES = 16
COL_TILES = 64


def draw_diag_inverse(key, part):
    key = jax.random.fold_in(key, 11)
    first, second = jax.random.split(key)
    lower = jax.random.normal(first, (TILE, TILE), jnp.float32)
    diagonal = jnp.exp(jax.random.uniform(second, (TILE,), jnp.float32, -0.69, 0.69))
    rows = jnp.arange(TILE, dtype=jnp.int32)[:, None]
    cols = jnp.arange(TILE, dtype=jnp.int32)[None, :]
    strict = jnp.where(cols < rows, lower * (1.0 / TILE ** 0.5), 0.0)
    return (strict + jnp.where(cols == rows, diagonal[:, None], 0.0)).astype(jnp.bfloat16)


def rank_levels(key, count):
    shifts = jax.random.randint(key, (count,), 0, 4)
    ranks = jnp.right_shift(jnp.full((count,), RANK_MAX, jnp.int32), shifts.astype(jnp.int32))
    ranks = ranks.at[0].set(RANK_MAX)
    return ranks.at[1].set(RANK_MAX // 8)


def draw_row_rank(key, part):
    key = jax.random.fold_in(key, 21)
    return rank_levels(key, ROW_TILES)


def draw_col_rank(key, part):
    key = jax.random.fold_in(key, 31)
    return rank_levels(key, COL_TILES)


def shard_levels(rng, extent, cuts, low, high):
    def one(position, shards_of):
        draws = jax.random.uniform(jax.random.fold_in(jax.random.fold_in(rng, 6), position), (shards_of,), jnp.float32, low / len(cuts), high / len(cuts))
        return jnp.repeat(jnp.exp(draws), extent[position] // shards_of).reshape((-1,) + (1,) * (len(extent) - position - 1))

    loudness = one(*cuts[0])
    for cut in cuts[1:]:
        loudness = loudness * one(*cut)
    return loudness


def scatter_about(stream_key, shape, spread, most, cuts=(), held_as=jnp.bfloat16):
    gain = shard_levels(stream_key, shape, cuts, -0.22, 0.18) if cuts else 1.0
    array = jax.random.normal(stream_key, shape, jnp.float32) * spread * gain
    return jnp.minimum(jnp.maximum(array, -most), most).astype(held_as)


def setup_inputs(seed: int = 0) -> dict:
    streams_of = jax.random.split(jax.random.key(seed), 6)
    return {
        "diag_inverse": draw_diag_inverse(jax.random.fold_in(streams_of[5], 71), 0),
        "row_v": scatter_about(streams_of[1], (ROW_TILES, TILE, RANK_MAX), 0.15, 0.8984375, ((0, 16), (1, 32))),
        "row_rank": draw_row_rank(jax.random.fold_in(streams_of[5], 71), 0),
        "col_v": scatter_about(streams_of[3], (COL_TILES, TILE, RANK_MAX), 0.15, 0.8984375, ((0, 32), (1, 16))),
        "col_rank": draw_col_rank(jax.random.fold_in(streams_of[5], 71), 0),
    }


def reference(diag_inverse, row_v, row_rank, col_v, col_rank):
    places = jnp.arange(RANK_MAX, dtype=jnp.int32)
    nothing = jnp.zeros((), jnp.bfloat16)
    row_masked = jnp.where(places[None, None, :] < row_rank[:, None, None], row_v, nothing)
    col_masked = jnp.where(places[None, None, :] < col_rank[:, None, None], col_v, nothing)
    inverse32 = diag_inverse.astype(jnp.float32)
    solved = jnp.einsum('ab,ibq->iaq', inverse32, row_masked.astype(jnp.float32)).astype(jnp.bfloat16)
    normal = jnp.einsum('ba,ibq->iaq', inverse32, solved.astype(jnp.float32)).astype(jnp.bfloat16)
    columns32 = col_masked.astype(jnp.float32)

    def one_row(normal_tile):
        return jnp.einsum('nq,jnp->jqp', normal_tile.astype(jnp.float32), columns32).astype(jnp.bfloat16)

    coupling = lax.map(one_row, normal)
    return solved, coupling
```

```python
import functools

import jax
import jax.numpy as jnp
from jax import lax
from jax.experimental import pallas as pl
from jax.experimental.pallas import tpu as pltpu
from jax.sharding import PartitionSpec as P

MESH = pl.DeviceIdType.MESH
TILE = 2048
RANK = 512
NX, NY, NZ = 4, 8, 8
ROWS = TILE // (NX * NZ)
HALF = ROWS // 2
CROWS = TILE // (2 * NY)
STREAMS = "VDCK"


def names():
    out = []
    out += [("Vz", s, h) for s, n in (("L", 4), ("S", 3)) for h in range(1, n + 1)]
    out += [("Vx", s, k) for s in ("L1", "L2", "S1") for k in range(8)]
    out += [("Dx", s) for s in ("L1", "L2", "S1")]
    out += [("Dz", x0, s, h) for x0 in range(4) for s, n in (("L", 4), ("S", 3)) for h in range(1, n + 1)]
    out += [("Ds", x0, k) for x0 in range(4) for k in range(8)]
    out += [("Cy", s, h) for s, n in (("L", 4), ("S", 3)) for h in range(1, n + 1)]
    out += [("Cs", k) for k in range(8)]
    return {n: i for i, n in enumerate(out)}


SEM = names()
HOPS = [None, ("L", 1), ("S", 1), ("L", 2), ("S", 2), ("L", 3), ("S", 3), ("L", 4)]


def kernel(dt_in, v_in, c_in, s_out, k_out, dt, v, c, vt, st, nt, send_sem, recv_sem, local_sem):
    row = lax.axis_index("row")
    col = lax.axis_index("col")
    core = row % 2
    y = row // 2
    x = col // NZ
    z = col % NZ
    d = 1 - 2 * core

    def at_z(step):
        return row, x * NZ + (z + step + NZ) % NZ

    def at_x(step):
        return row, ((x + step + NX) % NX) * NZ + z

    def at_y(step):
        return ((y + step + NY) % NY) * 2 + core, col

    sibling = (y * 2 + 1 - core, col)

    barrier = pltpu.get_barrier_semaphore()
    peers = (at_z(1), at_z(-1), at_x(1), at_x(-1), at_y(1), at_y(-1), sibling)
    for peer in peers:
        pl.semaphore_signal(barrier, inc=1, device_id=peer, device_id_type=MESH)
    pl.semaphore_wait(barrier, len(peers))

    copies = {}

    def send(name, src, dst, to):
        i = SEM[name]
        copy = pltpu.make_async_remote_copy(
            src_ref=src, dst_ref=dst, send_sem=send_sem.at[i], recv_sem=recv_sem.at[i],
            device_id=to, device_id_type=MESH,
        )
        copy.start()
        copies[name] = copy

    def got(name):
        copies[name].wait_recv()

    def vblock(xx, zz):
        return v.at[pl.ds(pl.multiple_of((xx * NZ + zz) * ROWS, ROWS), ROWS)]

    def dblock(xx, zz, first=0):
        rows = pl.ds(pl.multiple_of((xx * NZ + zz) * ROWS + core * HALF, HALF), HALF)
        return dt.at[rows, first:]

    def cblock(yy):
        return c.at[:, pl.ds(pl.multiple_of((yy * 2 + core) * CROWS, CROWS), CROWS)]

    def zz_of(k):
        if HOPS[k] is None:
            return z
        s, h = HOPS[k]
        return (z - d * h + NZ) % NZ if s == "L" else (z + d * h + NZ) % NZ

    def yy_of(k):
        if HOPS[k] is None:
            return y
        s, h = HOPS[k]
        return (y - d * h + NY) % NY if s == "L" else (y + d * h + NY) % NY

    xm = (x - d + NX) % NX

    own_d = dt_in.at[pl.ds(pl.multiple_of(core * HALF, HALF), HALF)]
    local = [
        pltpu.make_async_copy(own_d, dblock(x, z), local_sem.at[0]),
        pltpu.make_async_copy(v_in, vblock(x, z), local_sem.at[1]),
        pltpu.make_async_copy(c_in, cblock(y), local_sem.at[2]),
    ]
    for copy in local:
        copy.start()

    if "D" in STREAMS:
        send(("Dx", "L1"), own_d, dblock(x, z), at_x(d))
        send(("Dx", "S1"), own_d, dblock(x, z), at_x(-d))
    if "V" in STREAMS:
        send(("Vz", "L", 1), v_in, vblock(x, z), at_z(d))
        send(("Vz", "S", 1), v_in, vblock(x, z), at_z(-d))
        send(("Vx", "L1", 0), v_in, vblock(x, z), at_x(d))
        send(("Vx", "S1", 0), v_in, vblock(x, z), at_x(-d))
    if "C" in STREAMS:
        send(("Cy", "L", 1), c_in, cblock(y), at_y(d))
        send(("Cy", "S", 1), c_in, cblock(y), at_y(-d))
        send(("Cs", 0), c_in, cblock(y), sibling)

    def v_z(k):
        s, h = HOPS[k]
        got(("Vz", s, h))
        zz = zz_of(k)
        if (s, h) not in (("L", 4), ("S", 3)):
            send(("Vz", s, h + 1), vblock(x, zz), vblock(x, zz), at_z(d if s == "L" else -d))
        send(("Vx", "L1", k), vblock(x, zz), vblock(x, zz), at_x(d))
        send(("Vx", "S1", k), vblock(x, zz), vblock(x, zz), at_x(-d))

    def v_x(k):
        got(("Vx", "L1", k))
        b = vblock(xm, zz_of(k))
        send(("Vx", "L2", k), b, b, at_x(d))

    def c_y(k):
        s, h = HOPS[k]
        got(("Cy", s, h))
        b = cblock(yy_of(k))
        if (s, h) not in (("L", 4), ("S", 3)):
            send(("Cy", s, h + 1), b, b, at_y(d if s == "L" else -d))
        send(("Cs", k), b, b, sibling)

    def d_x1():
        got(("Dx", "L1"))
        b = dblock(xm, z)
        send(("Dx", "L2"), b, b, at_x(d))

    def d_x2():
        got(("Dx", "S1"))
        got(("Dx", "L2"))
        for x0 in range(4):
            b = dblock(x0, z, 512 * x0)
            send(("Dz", x0, "L", 1), b, b, at_z(d))
            send(("Dz", x0, "S", 1), b, b, at_z(-d))
        for x0 in range(4):
            b = dblock(x0, z, 512 * x0)
            send(("Ds", x0, 0), b, b, sibling)

    def d_z(x0, k):
        s, h = HOPS[k]
        got(("Dz", x0, s, h))
        b = dblock(x0, zz_of(k), 512 * x0)
        if (s, h) not in (("L", 4), ("S", 3)):
            send(("Dz", x0, s, h + 1), b, b, at_z(d if s == "L" else -d))
        send(("Ds", x0, k), b, b, sibling)

    V, D, C = "V" in STREAMS, "D" in STREAMS, "C" in STREAMS
    for copy in local:
        copy.wait()
    if V:
        v_z(1), v_z(2)
    if D:
        d_x1()
    if V:
        v_z(3), v_z(4)
    if C:
        c_y(1), c_y(2)
    if V:
        v_x(0), v_x(1), v_x(2)
    if D:
        d_x2()
    if V:
        v_z(5), v_z(6), v_z(7)
        v_x(3), v_x(4)
    if D:
        for x0 in range(4):
            d_z(x0, 1), d_z(x0, 2)
    if C:
        c_y(3), c_y(4)
    if V:
        v_x(5), v_x(6), v_x(7)
    if D:
        for x0 in range(4):
            d_z(x0, 3), d_z(x0, 4)
    if C:
        c_y(5), c_y(6)
    if D:
        for x0 in range(4):
            d_z(x0, 5), d_z(x0, 6)
    if C:
        c_y(7)
    if D:
        for x0 in range(4):
            d_z(x0, 7)
    if V:
        for k in range(8):
            got(("Vx", "S1", k)), got(("Vx", "L2", k))
    if D:
        for x0 in range(4):
            for k in range(8):
                got(("Ds", x0, k))
    if C:
        for k in range(8):
            got(("Cs", k))

    if "K" in STREAMS:
        vt[...] = v[...].T

        for a in range(0, TILE, 256):
            e = a + 256
            st[:, a:e] = jnp.dot(
                vt[:, :e], dt[:e, a:e], preferred_element_type=jnp.float32
            ).astype(jnp.bfloat16)
        for a in range(0, TILE, 256):
            e = a + 256
            nt[:, a:e] = lax.dot_general(
                st[:, a:], dt[a:e, a:], (((1,), (1,)), ((), ())), preferred_element_type=jnp.float32
            ).astype(jnp.bfloat16)
        for j in range(2):
            for p in range(0, RANK, 256):
                k_out[j, :, p:p + 256] = jnp.dot(
                    nt[...], c[j, :, p:p + 256], preferred_element_type=jnp.float32
                ).astype(jnp.bfloat16)
        pair = pl.multiple_of((col // 2) * 2 * ROWS, 2 * ROWS)
        both = st[:, pl.ds(pair, 2 * ROWS)].T
        s_out[...] = jnp.where(col % 2 == 0, both[:ROWS], both[ROWS:])
    else:
        s_out[...] = v[:ROWS]
        k_out[...] = c[:, :RANK]

    for copy in copies.values():
        copy.wait_send()


def on_device(diag_inverse, row_v, row_rank, col_v, col_rank):
    vmem = pl.BlockSpec(memory_space=pltpu.VMEM)
    hbm = pl.BlockSpec(memory_space=pltpu.HBM)
    solved, cores = pl.pallas_call(
        kernel,
        out_shape=(
            jax.ShapeDtypeStruct((ROWS, RANK), jnp.bfloat16),
            jax.ShapeDtypeStruct((2, RANK, RANK), jnp.bfloat16),
        ),
        in_specs=[hbm] * 3,
        out_specs=(vmem, vmem),
        scratch_shapes=[
            pltpu.VMEM((TILE, TILE), jnp.bfloat16),
            pltpu.VMEM((TILE, RANK), jnp.bfloat16),
            pltpu.VMEM((2, TILE, RANK), jnp.bfloat16),
            pltpu.VMEM((RANK, TILE), jnp.bfloat16),
            pltpu.VMEM((RANK, TILE), jnp.bfloat16),
            pltpu.VMEM((RANK, TILE), jnp.bfloat16),
            pltpu.SemaphoreType.DMA((len(SEM),)),
            pltpu.SemaphoreType.DMA((len(SEM),)),
            pltpu.SemaphoreType.DMA((3,)),
        ],
        compiler_params=pltpu.CompilerParams(
            collective_id=0, has_side_effects=True, vmem_limit_bytes=48 * 1024 * 1024
        ),
    )(diag_inverse.T, row_v[0], col_v)
    places = jnp.arange(RANK, dtype=jnp.int32)
    nothing = jnp.zeros((), jnp.bfloat16)
    rows = places < row_rank[0]
    cols = places[None, :] < col_rank[:, None]
    solved = jnp.where(rows[None, :], solved, nothing)
    cores = jnp.where(rows[None, :, None] & cols[:, None, :], cores, nothing)
    return solved[None], cores[None]


def solution(mesh):
    in_specs = (P(None, "col"), P("row", "col", None), P("row"), P("col", "row", None), P("col"))
    out_specs = (P("row", "col", None), P("row", "col", None, None))
    return jax.shard_map(
        on_device, mesh=mesh, in_specs=in_specs, out_specs=out_specs, check_vma=False
    )
```

```python
import jax
import jax.numpy as jnp
from jax import lax
from jax.experimental import pallas as pl
from jax.experimental.pallas import tpu as pltpu
from jax.sharding import PartitionSpec as P

MESH = pl.DeviceIdType.MESH
BF16 = jnp.bfloat16
F32 = jnp.float32
TILE = 2048
RANK = 512
NX, NY, NZ = 4, 8, 8
ROWS = TILE // (NX * NZ)
HALF = ROWS // 2
GROUP = TILE // NX
CROWS = TILE // (2 * NY)
TAIL = 384
BODY = TILE - TAIL
BODY_ROWS = TILE - GROUP
PIECES = 2
DIRECT = ()
HOPS = ((), ("L", 1), ("S", 1), ("L", 2), ("S", 2), ("L", 3), ("S", 3), ("L", 4))
WAYS = (("L", 4), ("S", 3))

ORDER = (
    1000, 1, 87, 68, 79, 24, 5, 1001, 72, -1, 2, 80, 9, 88, -35, -68, -34, 50, 69, -5, 54, 57, 6, 8, 25, -32, 10,
    -33, 61, 47, -72, 40, -79, 81, 43, 26, -87, -2, 3, 36, 89, 73, -6, -50, 11, -54, -69, -80, 7, 82, -57, 27, -88,
    55, -61, 58, 12, 62, -10, 18, -47, 70, -43, 44, 28, 90, -3, 51, 4, 13, -81, -73, 29, -8, -11, 83, 48, -40, -36,
    74, -58, -89, 37, -55, -7, 14, 16, -62, -82, 84, 30, 59, -12, -44, -70, 56, 63, -51, -9, 17, 52, 19, 41, 91, 71,
    -13, -4, 45, 31, 15, -83, -48, 49, 20, -59, 21, 85, -90, -37, 38, -74, -52, -63, 60, -14, 53, -84, -56, -71, 86,
    75, -41, 42, -45, -15, 46, -95, 2000, -91, 22, 23, 92, 2001, -38, 39, -60, 77, -85, -49, -53, 93, -75, 66, -86,
    76, -42, -46, 65, -93, -39, 64, 67, -96, -92, -65, -66, 2002, 2003, 94, -64, 2004, 2005, -77, 2006, 2008, -76,
    78, 2007, 2009, -67, -94, -78, 2010,
)
TASKS = tuple(("T", m) for m in range(NX)) + tuple((s, b) for b in range(NX - 1) for s in ("S", "N")) + (("P", 3),)


def copy_names():
    out = [("Vz", s, h) for s, n in WAYS for h in range(1, n + 1)]
    out += [("Vx", s, k) for s in ("L1", "L2", "S1") for k in range(NZ)]
    out += [("Dx", x0) for x0 in range(NX)]
    out += [("Dz", x0, s, h) for x0 in range(NX) for s, n in WAYS for h in range(1, n + 1)]
    out += [("Ds", x0) for x0 in range(NX)]
    out += [("Az", s, h) for s, n in WAYS for h in range(1, n + 1)]
    out += [("Ax", s) for s in ("L1", "L2", "S1")] + [("As", 0)]
    out += [("Cy", s, h, j) for s, n in WAYS for h in range(1, n + 1) for j in range(PIECES)]
    out += [("Cs", j) for j in range(PIECES)]
    out += [("Vx", "S1"), ("Vx", "L2")]
    return out


NAMES = [None] + copy_names()
SEM = {n: i - 1 for i, n in enumerate(NAMES) if i}
SENT = {"V": 0, "A": 1, "As": 2, "own": 3, "D": 4, "Cy": 8, "Cs": 10}
WIDE = 12


def kernel(
    dt_in, v_in, row_rank, c_in, col_rank_in, s_out, k_out, dt, v, c, vt, st, nt, na, sa, col_rank,
    send_sem, recv_sem, local_sem, rank_sem,
):
    row = lax.axis_index("row")
    col = lax.axis_index("col")
    core = lax.rem(row, 2)
    y = lax.div(row, 2)
    x = lax.div(col, NZ)
    z = lax.rem(col, NZ)
    d = 1 - 2 * core

    def around(at, step, n):
        return lax.rem(at + step + n, n)

    def at_z(step):
        return row, x * NZ + around(z, step, NZ)

    def at_x(step):
        return row, around(x, step, NX) * NZ + z

    def at_y(step):
        return around(y, step, NY) * 2 + core, col

    sibling = (y * 2 + 1 - core, col)
    to_z = {"L": at_z(d), "S": at_z(-d)}
    to_y = {"L": at_y(d), "S": at_y(-d)}
    to_x = {"L1": at_x(d), "L2": at_x(d), "S1": at_x(-d), "X2": at_x(2)}
    near_z, near_y = [z], [y]
    for s, h in HOPS[1:]:
        near_z.append(around(z, -d * h if s == "L" else d * h, NZ))
        near_y.append(around(y, -d * h if s == "L" else d * h, NY))
    x_from = (x, around(x, -d, NX), around(x, d, NX), around(x, 2, NX))

    barrier = pltpu.get_barrier_semaphore()
    peers = (*to_z.values(), to_x["L1"], to_x["S1"], to_x["X2"], *to_y.values(), sibling)
    for peer in peers:
        pl.semaphore_signal(barrier, inc=1, device_id=peer, device_id_type=MESH)
    pl.semaphore_wait(barrier, len(peers))

    half = pl.ds(pl.multiple_of(core * HALF, HALF), HALF)

    def body(x0):
        return pl.ds(GROUP * x0, BODY - GROUP * x0)

    tail = pl.ds(BODY, TAIL)

    def v_block(xx, zz):
        return v.at[pl.ds(pl.multiple_of((xx * NZ + zz) * ROWS, ROWS), ROWS)]

    def d_block(xx, zz, columns):
        return dt.at[xx * NZ + zz, half, columns]

    def c_block(yy, j):
        return c.at[j, yy, core] if PIECES == 2 else c.at[:, yy, core]

    def leaving(at, s, h):
        return at[0 if h == 1 else HOPS.index((s, h - 1))]

    def ends(name):
        kind = name[0]
        if kind == "Vz":
            s, h = name[1:]
            block = v_block(x, leaving(near_z, s, h))
            return (v_in if h == 1 else block), block, to_z[s], SENT["V"]
        if kind == "Vx":
            s, k = name[1:]
            if s == "L2" and k in DIRECT:
                s = "X2"
            block = v_block(x_from[1] if s == "L2" else x, near_z[k])
            return (v_in if k == 0 and s != "L2" else block), block, to_x[s], SENT["V"]
        if kind == "Dz":
            x0, s, h = name[1:]
            block = d_block(x0, leaving(near_z, s, h), body(x0))
            return block, block, to_z[s], SENT["D"] + x0
        if kind == "Ds":
            x0 = name[1]
            block = dt.at[pl.ds(x0 * NZ, NZ), half, body(x0)]
            return block, block, sibling, SENT["D"] + x0
        if kind == "Az":
            s, h = name[1:]
            block = d_block(x, leaving(near_z, s, h), tail)
            return (dt_in.at[half, tail] if h == 1 else block), block, to_z[s], SENT["A"]
        if kind == "Ax":
            s = name[1]
            xx = x_from[1] if s == "L2" else x
            block = dt.at[pl.ds(xx * NZ, NZ), half, tail]
            return block, block, to_x[s], SENT["A"]
        if kind == "As":
            block = dt.at[:, half, tail]
            return block, block, sibling, SENT["As"]
        if kind == "Cy":
            s, h, j = name[1:]
            block = c_block(leaving(near_y, s, h), j)
            src = block if h > 1 else (c_in.at[j] if PIECES == 2 else c_in)
            return src, block, to_y[s], SENT["Cy"] + j
        j = name[1]
        block = c.at[j, :, core] if PIECES == 2 else c.at[:, :, core]
        return block, block, sibling, SENT["Cs"] + j

    def arrival(name):
        if name[0] == "Vx" and name[1] in ("S1", "L2"):
            return recv_sem.at[SEM[name[:2]]]
        return recv_sem.at[SEM[name]]

    def start(name):
        src, dst, to, sent = ends(name)
        pltpu.make_async_remote_copy(
            src_ref=src, dst_ref=dst, send_sem=send_sem.at[sent], recv_sem=arrival(name),
            device_id=to, device_id_type=MESH,
        ).start()

    def wait_bytes(ref, sem):
        pltpu.make_async_copy(ref, ref, sem).wait()

    def wait(name):
        if len(name) == 2 and name[0] == "Vx":
            ref = v.at[pl.ds(0, NZ * ROWS)]
        elif name[0] == "Dx":
            ref = d_block(name[1], z, body(name[1]))
        else:
            ref = ends(name)[1]
        wait_bytes(ref, arrival(name))

    def start_own(x0, kind):
        src, dst = dt_in.at[half, body(x0)], d_block(x0, z, body(x0))
        if kind == "x":
            ways = [(to_x[s], SENT["own"], ("Dx", x0)) for s in ("L1", "S1", "X2")]
        else:
            ways = [(to_z[s], SENT["D"] + x0, ("Dz", x0, s, 1)) for s in ("L", "S")]
        for to, sent, name in ways:
            pltpu.make_async_remote_copy(
                src_ref=src, dst_ref=dst, send_sem=send_sem.at[sent], recv_sem=arrival(name),
                device_id=to, device_id_type=MESH,
            ).start()

    def finish_sends():
        wait_bytes(v.at[pl.ds(0, 31 * ROWS)], send_sem.at[SENT["V"]])
        for x0 in range(NX):
            wait_bytes(dt.at[pl.ds(0, 15), pl.ds(0, HALF), body(x0)], send_sem.at[SENT["D"] + x0])
        if TAIL:
            wait_bytes(dt.at[pl.ds(0, 31), pl.ds(0, HALF), tail], send_sem.at[SENT["A"]])
            wait_bytes(dt.at[:, half, tail], send_sem.at[SENT["As"]])
        for j in range(PIECES):
            ring = c.at[j, pl.ds(0, 7), 0] if PIECES == 2 else c.at[:, pl.ds(0, 7), 0]
            wait_bytes(ring, send_sem.at[SENT["Cy"] + j])
            across = c.at[j, :, core] if PIECES == 2 else c.at[:, :, core]
            wait_bytes(across, send_sem.at[SENT["Cs"] + j])
        for x0 in range(NX):
            only_here(
                x0, True,
                lambda x0=x0: wait_bytes(dt.at[pl.ds(0, 3), pl.ds(0, HALF), body(x0)], send_sem.at[SENT["own"]]),
            )

    local = [
        pltpu.make_async_copy(dt_in.at[half], d_block(x, z, pl.ds(0, TILE)), local_sem.at[0]),
        pltpu.make_async_copy(v_in, v_block(x, z), local_sem.at[1]),
    ]
    local += [
        pltpu.make_async_copy(c_in.at[j] if PIECES == 2 else c_in, c_block(y, j), local_sem.at[2 + j])
        for j in range(PIECES)
    ]

    ranks = [
        pltpu.make_async_copy(col_rank_in, col_rank, rank_sem.at[0]),
    ]

    def finish_local():
        for one in local:
            one.wait()

    def only_here(x0, here, make):
        @pl.when(x == x0 if here else x != x0)
        def _():
            make()

    def compute(task):
        kind, b = task
        if kind == "T":
            first = pl.multiple_of(x_from[b] * GROUP, GROUP)
            vt[:, pl.ds(first, GROUP)] = v[pl.ds(first, GROUP)].T
            return
        if kind == "P":
            for a in range(0, GROUP, 256):
                columns = dt[:BODY_ROWS // ROWS, :, BODY_ROWS + a:BODY_ROWS + a + 256]
                sa[:, a:a + 256] = jnp.dot(
                    vt[:, :BODY_ROWS], columns.reshape(BODY_ROWS, 256), preferred_element_type=F32
                )
            return
        lo, hi = GROUP * b, GROUP * (b + 1)
        if kind == "S":
            for a in range(lo, hi, 256):
                e = min(a + 256, hi)
                st[:, a:e] = jnp.dot(
                    vt[:, :hi], dt[:hi // ROWS, :, a:e].reshape(hi, e - a), preferred_element_type=F32
                ).astype(BF16)
            return
        for a in range(0, hi, 256):
            e = a + 256
            part = lax.dot_general(
                st[:, lo:hi], dt[a // ROWS:e // ROWS, :, lo:hi].reshape(256, GROUP),
                (((1,), (1,)), ((), ())), preferred_element_type=F32,
            )
            if b < NX - 1:
                na[:, a:e] = part if a >= lo else na[:, a:e] + part
            else:
                nt[:, a:e] = (part if a >= lo else na[:, a:e] + part).astype(BF16)

    def finish():
        for a in range(0, GROUP, 256):
            e = BODY_ROWS + a
            last = dt[BODY_ROWS // ROWS:, :, e:e + 256].reshape(GROUP, 256)
            part = jnp.dot(vt[:, BODY_ROWS:], last, preferred_element_type=F32)
            st[:, e:e + 256] = (sa[:, a:a + 256] + part).astype(BF16)
        compute(("N", NX - 1))
        pair = pl.multiple_of((col // 2) * 2 * ROWS, 2 * ROWS)
        both = st[:, pl.ds(pair, 2 * ROWS)].T
        mine = jnp.where(col % 2 == 0, both[:ROWS], both[ROWS:])
        for one in ranks:
            one.wait()
        q = lax.broadcasted_iota(jnp.int32, (ROWS, RANK), 1)
        s_out[...] = jnp.where(q < row_rank[0], mine.astype(F32), 0.0).astype(BF16)
        q = lax.broadcasted_iota(jnp.int32, (RANK, 256), 0)
        p = lax.broadcasted_iota(jnp.int32, (RANK, 256), 1)
        for j in range(2):
            for first in range(0, RANK, 256):
                columns = c[j, :, :, :, first:first + 256].reshape(TILE, 256)
                part = jnp.dot(nt[...], columns, preferred_element_type=F32)
                kept = (q < row_rank[0]) & (p < col_rank[j] - first)
                k_out[j, :, first:first + 256] = jnp.where(kept, part, 0.0).astype(BF16)

    here = False
    for code in ORDER:
        if code in (1000, 1001):
            for x0 in range(NX):
                only_here(x0, True, lambda x0=x0: start_own(x0, "xz"[code - 1000]))
        elif code >= 2000:
            compute(TASKS[code - 2000])
        elif code > 0:
            name = NAMES[code]
            if name[0] == "Dz" and name[3] == 1:
                only_here(name[1], False, lambda name=name: start(name))
            else:
                start(name)
        else:
            if not here:
                for one in local + ranks:
                    one.start()
                finish_local()
                here = True
            name = NAMES[-code]
            if name[0] == "Dx":
                only_here(name[1], False, lambda name=name: wait(name))
            else:
                wait(name)

    finish()
    finish_sends()


VMEM_LIMIT = 48 * 1024 * 1024


def in_hbm(array):
    return pltpu.with_memory_space_constraint(array, pltpu.HBM)


def on_device(diag_inverse, row_v, row_rank, col_v, col_rank):
    vmem = pl.BlockSpec(memory_space=pltpu.VMEM)
    hbm = pl.BlockSpec(memory_space=pltpu.HBM)
    smem = pl.BlockSpec(memory_space=pltpu.SMEM)
    solved, cores = pl.pallas_call(
        kernel,
        out_shape=(
            pltpu.VMEM((ROWS, RANK), BF16),
            pltpu.VMEM((2, RANK, RANK), BF16),
        ),
        in_specs=[hbm, hbm, smem, hbm, hbm],
        out_specs=(vmem, vmem),
        scratch_shapes=[
            pltpu.VMEM((NX * NZ, ROWS, TILE), BF16),
            pltpu.VMEM((TILE, RANK), BF16),
            pltpu.VMEM((2, NY, 2, CROWS, RANK), BF16),
            pltpu.VMEM((RANK, TILE), BF16),
            pltpu.VMEM((RANK, TILE), BF16),
            pltpu.VMEM((RANK, TILE), BF16),
            pltpu.VMEM((RANK, TILE), F32),
            pltpu.VMEM((RANK, GROUP), F32),
            pltpu.SMEM((2,), jnp.int32),
            pltpu.SemaphoreType.DMA((WIDE,)),
            pltpu.SemaphoreType.DMA((len(SEM),)),
            pltpu.SemaphoreType.DMA((4,)),
            pltpu.SemaphoreType.DMA((1,)),
        ],
        compiler_params=pltpu.CompilerParams(
            collective_id=0, has_side_effects=True, vmem_limit_bytes=VMEM_LIMIT
        ),
    )(in_hbm(diag_inverse.T), in_hbm(row_v[0]), row_rank, in_hbm(col_v), in_hbm(col_rank))
    return solved[None], cores[None]


def solution(mesh):
    in_specs = (P(None, "col"), P("row", "col", None), P("row"), P("col", "row", None), P("col"))
    out_specs = (P("row", "col", None), P("row", "col", None, None))
    return jax.shard_map(
        on_device, mesh=mesh, in_specs=in_specs, out_specs=out_specs, check_vma=False
    )
```

```python
import jax
import jax.numpy as jnp
from jax import lax
from jax.experimental import pallas as pl
from jax.experimental.pallas import tpu as pltpu
from jax.sharding import PartitionSpec as P

MESH = pl.DeviceIdType.MESH
BF16 = jnp.bfloat16
F32 = jnp.float32
TILE = 2048
RANK = 512
NX, NY, NZ = 4, 8, 8
ROWS = TILE // (NX * NZ)
HALF = ROWS // 2
GROUP = TILE // NX
CROWS = TILE // (2 * NY)
TAIL = 384
BODY = TILE - TAIL
BODY_ROWS = TILE - GROUP
PIECES = 2
DIRECT = (0, 7,)
HOPS = ((), ("L", 1), ("S", 1), ("L", 2), ("S", 2), ("L", 3), ("S", 3), ("L", 4))
WAYS = (("L", 4), ("S", 3))

ORDER = (
    1000, 1, 24, 87, 68, 79, 16, 88, 5, 80, 1001, 72, -35, 61, 57, -1, 2, 9, -34, 50, -5, 6, 10, 8, -68, 54, -33,
    69, 43, 25, -32, -87, 36, 89, -79, -57, 26, 58, -72, 40, 81, 47, -2, 3, 73, 11, -80, -6, 82, 28, -69, 12, 7,
    -50, 51, -9, -61, -88, 90, 62, -10, -43, 18, 27, 70, -36, 17, 44, 37, -47, -58, -11, 19, -89, -81, 83, -3, 4,
    -40, -54, 29, 59, 13, -73, -51, 48, -62, -12, 41, -82, 84, -90, 20, -70, 74, -7, 92, 71, 30, -44, 14, 45, 63,
    91, 55, -37, 52, -4, 31, 38, -59, 23, 15, -83, 85, -13, -41, -48, 42, -71, -74, 75, 49, 21, -55, -45, -14, 46,
    -84, -8, 86, -38, 39, 22, -92, -15, -52, 53, -63, -95, 2000, 77, -91, 56, -42, -85, 93, 60, 2002, -49, -46, 65,
    -75, 76, -39, 64, -93, -53, 2001, -56, -65, -60, -86, 67, -96, 2003, 66, 94, -64, 2004, 2005, 2006, -66, -77,
    2008, -76, 78, 2007, -67, -94, 2009, -78, 2010,
)
TASKS = tuple(("T", m) for m in range(NX)) + tuple((s, b) for b in range(NX - 1) for s in ("S", "N")) + (("P", 3),)


def copy_names():
    out = [("Vz", s, h) for s, n in WAYS for h in range(1, n + 1)]
    out += [("Vx", s, k) for s in ("L1", "L2", "S1") for k in range(NZ)]
    out += [("Dx", x0) for x0 in range(NX)]
    out += [("Dz", x0, s, h) for x0 in range(NX) for s, n in WAYS for h in range(1, n + 1)]
    out += [("Ds", x0) for x0 in range(NX)]
    out += [("Az", s, h) for s, n in WAYS for h in range(1, n + 1)]
    out += [("Ax", s) for s in ("L1", "L2", "S1")] + [("As", 0)]
    out += [("Cy", s, h, j) for s, n in WAYS for h in range(1, n + 1) for j in range(PIECES)]
    out += [("Cs", j) for j in range(PIECES)]
    out += [("Vx", "S1"), ("Vx", "L2")]
    return out


NAMES = [None] + copy_names()
SEM = {n: i - 1 for i, n in enumerate(NAMES) if i}
SENT = {"V": 0, "A": 1, "As": 2, "own": 3, "D": 4, "Cy": 8, "Cs": 10}
WIDE = 12


def kernel(
    dt_in, v_in, row_rank, c_in, col_rank_in, s_out, k_out, dt, v, c, vt, st, nt, na, sa, col_rank,
    send_sem, recv_sem, local_sem, rank_sem,
):
    row = lax.axis_index("row")
    col = lax.axis_index("col")
    core = lax.rem(row, 2)
    y = lax.div(row, 2)
    x = lax.div(col, NZ)
    z = lax.rem(col, NZ)
    d = 1 - 2 * core

    def around(at, step, n):
        return lax.rem(at + step + n, n)

    def at_z(step):
        return row, x * NZ + around(z, step, NZ)

    def at_x(step):
        return row, around(x, step, NX) * NZ + z

    def at_y(step):
        return around(y, step, NY) * 2 + core, col

    sibling = (y * 2 + 1 - core, col)
    to_z = {"L": at_z(d), "S": at_z(-d)}
    to_y = {"L": at_y(d), "S": at_y(-d)}
    to_x = {"L1": at_x(d), "L2": at_x(d), "S1": at_x(-d), "X2": at_x(2)}
    near_z, near_y = [z], [y]
    for s, h in HOPS[1:]:
        near_z.append(around(z, -d * h if s == "L" else d * h, NZ))
        near_y.append(around(y, -d * h if s == "L" else d * h, NY))
    x_from = (x, around(x, -d, NX), around(x, d, NX), around(x, 2, NX))

    barrier = pltpu.get_barrier_semaphore()
    peers = (*to_z.values(), to_x["L1"], to_x["S1"], to_x["X2"], *to_y.values(), sibling)
    for peer in peers:
        pl.semaphore_signal(barrier, inc=1, device_id=peer, device_id_type=MESH)
    pl.semaphore_wait(barrier, len(peers))

    half = pl.ds(pl.multiple_of(core * HALF, HALF), HALF)

    def body(x0):
        return pl.ds(GROUP * x0, BODY - GROUP * x0)

    tail = pl.ds(BODY, TAIL)

    def v_block(xx, zz):
        return v.at[pl.ds(pl.multiple_of((xx * NZ + zz) * ROWS, ROWS), ROWS)]

    def d_block(xx, zz, columns):
        return dt.at[xx * NZ + zz, half, columns]

    def c_block(yy, j):
        return c.at[j, yy, core] if PIECES == 2 else c.at[:, yy, core]

    def leaving(at, s, h):
        return at[0 if h == 1 else HOPS.index((s, h - 1))]

    def ends(name):
        kind = name[0]
        if kind == "Vz":
            s, h = name[1:]
            block = v_block(x, leaving(near_z, s, h))
            return (v_in if h == 1 else block), block, to_z[s], SENT["V"]
        if kind == "Vx":
            s, k = name[1:]
            if s == "L2" and k in DIRECT:
                s = "X2"
            block = v_block(x_from[1] if s == "L2" else x, near_z[k])
            return (v_in if k == 0 and s != "L2" else block), block, to_x[s], SENT["V"]
        if kind == "Dz":
            x0, s, h = name[1:]
            block = d_block(x0, leaving(near_z, s, h), body(x0))
            return block, block, to_z[s], SENT["D"] + x0
        if kind == "Ds":
            x0 = name[1]
            block = dt.at[pl.ds(x0 * NZ, NZ), half, body(x0)]
            return block, block, sibling, SENT["D"] + x0
        if kind == "Az":
            s, h = name[1:]
            block = d_block(x, leaving(near_z, s, h), tail)
            return (dt_in.at[half, tail] if h == 1 else block), block, to_z[s], SENT["A"]
        if kind == "Ax":
            s = name[1]
            xx = x_from[1] if s == "L2" else x
            block = dt.at[pl.ds(xx * NZ, NZ), half, tail]
            return block, block, to_x[s], SENT["A"]
        if kind == "As":
            block = dt.at[:, half, tail]
            return block, block, sibling, SENT["As"]
        if kind == "Cy":
            s, h, j = name[1:]
            block = c_block(leaving(near_y, s, h), j)
            src = block if h > 1 else (c_in.at[j] if PIECES == 2 else c_in)
            return src, block, to_y[s], SENT["Cy"] + j
        j = name[1]
        block = c.at[j, :, core] if PIECES == 2 else c.at[:, :, core]
        return block, block, sibling, SENT["Cs"] + j

    def arrival(name):
        if name[0] == "Vx" and name[1] in ("S1", "L2"):
            return recv_sem.at[SEM[name[:2]]]
        return recv_sem.at[SEM[name]]

    def start(name):
        src, dst, to, sent = ends(name)
        pltpu.make_async_remote_copy(
            src_ref=src, dst_ref=dst, send_sem=send_sem.at[sent], recv_sem=arrival(name),
            device_id=to, device_id_type=MESH,
        ).start()

    def wait_bytes(ref, sem):
        pltpu.make_async_copy(ref, ref, sem).wait()

    def wait(name):
        if len(name) == 2 and name[0] == "Vx":
            ref = v.at[pl.ds(0, NZ * ROWS)]
        elif name[0] == "Dx":
            ref = d_block(name[1], z, body(name[1]))
        else:
            ref = ends(name)[1]
        wait_bytes(ref, arrival(name))

    def start_own(x0, kind):
        src, dst = dt_in.at[half, body(x0)], d_block(x0, z, body(x0))
        if kind == "x":
            ways = [(to_x[s], SENT["own"], ("Dx", x0)) for s in ("L1", "S1", "X2")]
        else:
            ways = [(to_z[s], SENT["D"] + x0, ("Dz", x0, s, 1)) for s in ("L", "S")]
        for to, sent, name in ways:
            pltpu.make_async_remote_copy(
                src_ref=src, dst_ref=dst, send_sem=send_sem.at[sent], recv_sem=arrival(name),
                device_id=to, device_id_type=MESH,
            ).start()

    def finish_sends():
        wait_bytes(v.at[pl.ds(0, 31 * ROWS)], send_sem.at[SENT["V"]])
        for x0 in range(NX):
            wait_bytes(dt.at[pl.ds(0, 15), pl.ds(0, HALF), body(x0)], send_sem.at[SENT["D"] + x0])
        if TAIL:
            wait_bytes(dt.at[pl.ds(0, 31), pl.ds(0, HALF), tail], send_sem.at[SENT["A"]])
            wait_bytes(dt.at[:, half, tail], send_sem.at[SENT["As"]])
        for j in range(PIECES):
            ring = c.at[j, pl.ds(0, 7), 0] if PIECES == 2 else c.at[:, pl.ds(0, 7), 0]
            wait_bytes(ring, send_sem.at[SENT["Cy"] + j])
            across = c.at[j, :, core] if PIECES == 2 else c.at[:, :, core]
            wait_bytes(across, send_sem.at[SENT["Cs"] + j])
        for x0 in range(NX):
            only_here(
                x0, True,
                lambda x0=x0: wait_bytes(dt.at[pl.ds(0, 3), pl.ds(0, HALF), body(x0)], send_sem.at[SENT["own"]]),
            )

    local = [
        pltpu.make_async_copy(dt_in.at[half], d_block(x, z, pl.ds(0, TILE)), local_sem.at[0]),
        pltpu.make_async_copy(v_in, v_block(x, z), local_sem.at[1]),
    ]
    local += [
        pltpu.make_async_copy(c_in.at[j] if PIECES == 2 else c_in, c_block(y, j), local_sem.at[2 + j])
        for j in range(PIECES)
    ]

    ranks = [
        pltpu.make_async_copy(col_rank_in, col_rank, rank_sem.at[0]),
    ]

    def finish_local():
        for one in local:
            one.wait()

    def only_here(x0, here, make):
        @pl.when(x == x0 if here else x != x0)
        def _():
            make()

    def compute(task):
        kind, b = task
        if kind == "T":
            first = pl.multiple_of(x_from[b] * GROUP, GROUP)
            vt[:, pl.ds(first, GROUP)] = v[pl.ds(first, GROUP)].T
            return
        if kind == "P":
            for a in range(0, GROUP, 256):
                columns = dt[:BODY_ROWS // ROWS, :, BODY_ROWS + a:BODY_ROWS + a + 256]
                sa[:, a:a + 256] = jnp.dot(
                    vt[:, :BODY_ROWS], columns.reshape(BODY_ROWS, 256), preferred_element_type=F32
                )
            return
        lo, hi = GROUP * b, GROUP * (b + 1)
        if kind == "S":
            for a in range(lo, hi, 256):
                e = min(a + 256, hi)
                st[:, a:e] = jnp.dot(
                    vt[:, :hi], dt[:hi // ROWS, :, a:e].reshape(hi, e - a), preferred_element_type=F32
                ).astype(BF16)
            return
        for a in range(0, hi, 256):
            e = a + 256
            part = lax.dot_general(
                st[:, lo:hi], dt[a // ROWS:e // ROWS, :, lo:hi].reshape(256, GROUP),
                (((1,), (1,)), ((), ())), preferred_element_type=F32,
            )
            if b < NX - 1:
                na[:, a:e] = part if a >= lo else na[:, a:e] + part
            else:
                nt[:, a:e] = (part if a >= lo else na[:, a:e] + part).astype(BF16)

    def finish():
        for a in range(0, GROUP, 256):
            e = BODY_ROWS + a
            last = dt[BODY_ROWS // ROWS:, :, e:e + 256].reshape(GROUP, 256)
            part = jnp.dot(vt[:, BODY_ROWS:], last, preferred_element_type=F32)
            st[:, e:e + 256] = (sa[:, a:a + 256] + part).astype(BF16)
        compute(("N", NX - 1))
        pair = pl.multiple_of((col // 2) * 2 * ROWS, 2 * ROWS)
        both = st[:, pl.ds(pair, 2 * ROWS)].T
        mine = jnp.where(col % 2 == 0, both[:ROWS], both[ROWS:])
        for one in ranks:
            one.wait()
        q = lax.broadcasted_iota(jnp.int32, (ROWS, RANK), 1)
        s_out[...] = jnp.where(q < row_rank[0], mine.astype(F32), 0.0).astype(BF16)
        q = lax.broadcasted_iota(jnp.int32, (RANK, 256), 0)
        p = lax.broadcasted_iota(jnp.int32, (RANK, 256), 1)
        for j in range(2):
            for first in range(0, RANK, 256):
                columns = c[j, :, :, :, first:first + 256].reshape(TILE, 256)
                part = jnp.dot(nt[...], columns, preferred_element_type=F32)
                kept = (q < row_rank[0]) & (p < col_rank[j] - first)
                k_out[j, :, first:first + 256] = jnp.where(kept, part, 0.0).astype(BF16)

    here = False
    for code in ORDER:
        if code in (1000, 1001):
            for x0 in range(NX):
                only_here(x0, True, lambda x0=x0: start_own(x0, "xz"[code - 1000]))
        elif code >= 2000:
            compute(TASKS[code - 2000])
        elif code > 0:
            name = NAMES[code]
            if name[0] == "Dz" and name[3] == 1:
                only_here(name[1], False, lambda name=name: start(name))
            else:
                start(name)
        else:
            if not here:
                for one in local + ranks:
                    one.start()
                finish_local()
                here = True
            name = NAMES[-code]
            if name[0] == "Dx":
                only_here(name[1], False, lambda name=name: wait(name))
            else:
                wait(name)

    finish()
    finish_sends()


VMEM_LIMIT = 48 * 1024 * 1024


def in_hbm(array):
    return pltpu.with_memory_space_constraint(array, pltpu.HBM)


def on_device(diag_inverse, row_v, row_rank, col_v, col_rank):
    vmem = pl.BlockSpec(memory_space=pltpu.VMEM)
    hbm = pl.BlockSpec(memory_space=pltpu.HBM)
    smem = pl.BlockSpec(memory_space=pltpu.SMEM)
    solved, cores = pl.pallas_call(
        kernel,
        out_shape=(
            pltpu.VMEM((ROWS, RANK), BF16),
            pltpu.VMEM((2, RANK, RANK), BF16),
        ),
        in_specs=[hbm, hbm, smem, hbm, hbm],
        out_specs=(vmem, vmem),
        scratch_shapes=[
            pltpu.VMEM((NX * NZ, ROWS, TILE), BF16),
            pltpu.VMEM((TILE, RANK), BF16),
            pltpu.VMEM((2, NY, 2, CROWS, RANK), BF16),
            pltpu.VMEM((RANK, TILE), BF16),
            pltpu.VMEM((RANK, TILE), BF16),
            pltpu.VMEM((RANK, TILE), BF16),
            pltpu.VMEM((RANK, TILE), F32),
            pltpu.VMEM((RANK, GROUP), F32),
            pltpu.SMEM((2,), jnp.int32),
            pltpu.SemaphoreType.DMA((WIDE,)),
            pltpu.SemaphoreType.DMA((len(SEM),)),
            pltpu.SemaphoreType.DMA((4,)),
            pltpu.SemaphoreType.DMA((1,)),
        ],
        compiler_params=pltpu.CompilerParams(
            collective_id=0, has_side_effects=True, vmem_limit_bytes=VMEM_LIMIT
        ),
    )(in_hbm(diag_inverse.T), in_hbm(row_v[0]), row_rank, in_hbm(col_v), in_hbm(col_rank))
    return solved[None], cores[None]


def solution(mesh):
    in_specs = (P(None, "col"), P("row", "col", None), P("row"), P("col", "row", None), P("col"))
    out_specs = (P("row", "col", None), P("row", "col", None, None))
    return jax.shard_map(
        on_device, mesh=mesh, in_specs=in_specs, out_specs=out_specs, check_vma=False
    )
```

```python
import jax
import jax.numpy as jnp
from jax import lax
from jax.experimental import pallas as pl
from jax.experimental.pallas import tpu as pltpu
from jax.sharding import PartitionSpec as P

MESH = pl.DeviceIdType.MESH
BF16 = jnp.bfloat16
F32 = jnp.float32
TILE = 2048
RANK = 512
NX, NY, NZ = 4, 8, 8
ROWS = TILE // (NX * NZ)
HALF = ROWS // 2
GROUP = TILE // NX
CROWS = TILE // (2 * NY)
TAIL = 384
BODY = TILE - TAIL
BODY_ROWS = TILE - GROUP
PIECES = 2
DIRECT = (0, 7,)
HOPS = ((), ("L", 1), ("S", 1), ("L", 2), ("S", 2), ("L", 3), ("S", 3), ("L", 4))
WAYS = (("L", 4), ("S", 3))

ORDER = (
    1000, 1, 24, 87, 68, 79, 16, 88, 5, 80, 1001, 72, -35, 61, 57, -1, 2, 9, -34, 50, -5, 6, 10, 8, -68, 54, -33,
    69, 43, 25, -32, 36, -57, 26, -87, 89, 58, -72, -79, 40, 81, 47, -2, 3, 73, 11, -6, 28, -69, -80, 82, 12, 7,
    -50, 51, -9, -61, 62, -10, -43, -88, 90, 18, 27, 70, -36, 17, 44, 37, -47, -58, -11, 19, -3, 4, -40, -89, -81,
    83, -54, 29, 59, 13, -73, -51, 48, -62, -12, 41, 20, -70, 74, -82, 84, -7, -90, 92, 71, 30, -44, 14, 45, 63, 91,
    55, -37, 52, -4, 31, 38, -59, 23, 15, -13, -41, -48, -83, 85, 42, -71, -74, 75, 49, 21, -55, -45, -14, 46, -8,
    -38, 39, -84, 86, 22, -15, -52, 53, -63, -92, -95, 2000, 77, 56, -42, 60, -91, 2002, -49, -85, 93, -46, 65, -75,
    76, -39, 64, -93, -53, 2001, -56, -65, -60, 67, -96, 2003, 66, -86, 94, -64, 2004, 2005, 2006, -66, -77, 2008,
    -76, 78, 2007, -67, -94, 2009, -78, 2010,
)
TASKS = tuple(("T", m) for m in range(NX)) + tuple((s, b) for b in range(NX - 1) for s in ("S", "N")) + (("P", 3),)


def copy_names():
    out = [("Vz", s, h) for s, n in WAYS for h in range(1, n + 1)]
    out += [("Vx", s, k) for s in ("L1", "L2", "S1") for k in range(NZ)]
    out += [("Dx", x0) for x0 in range(NX)]
    out += [("Dz", x0, s, h) for x0 in range(NX) for s, n in WAYS for h in range(1, n + 1)]
    out += [("Ds", x0) for x0 in range(NX)]
    out += [("Az", s, h) for s, n in WAYS for h in range(1, n + 1)]
    out += [("Ax", s) for s in ("L1", "L2", "S1")] + [("As", 0)]
    out += [("Cy", s, h, j) for s, n in WAYS for h in range(1, n + 1) for j in range(PIECES)]
    out += [("Cs", j) for j in range(PIECES)]
    out += [("Vx", "S1"), ("Vx", "L2")]
    return out


NAMES = [None] + copy_names()
SEM = {n: i - 1 for i, n in enumerate(NAMES) if i}
SENT = {"V": 0, "A": 1, "As": 2, "own": 3, "D": 4, "Cy": 8, "Cs": 10}
WIDE = 12


def kernel(
    dt_in, v_in, row_rank, c_in, col_rank_in, s_out, k_out, dt, v, c, vt, st, nt, na, sa, col_rank,
    send_sem, recv_sem, local_sem, rank_sem,
):
    row = lax.axis_index("row")
    col = lax.axis_index("col")
    core = lax.rem(row, 2)
    y = lax.div(row, 2)
    x = lax.div(col, NZ)
    z = lax.rem(col, NZ)
    d = 1 - 2 * core

    def around(at, step, n):
        return lax.rem(at + step + n, n)

    def at_z(step):
        return row, x * NZ + around(z, step, NZ)

    def at_x(step):
        return row, around(x, step, NX) * NZ + z

    def at_y(step):
        return around(y, step, NY) * 2 + core, col

    sibling = (y * 2 + 1 - core, col)
    to_z = {"L": at_z(d), "S": at_z(-d)}
    to_y = {"L": at_y(d), "S": at_y(-d)}
    to_x = {"L1": at_x(d), "L2": at_x(d), "S1": at_x(-d), "X2": at_x(2)}
    near_z, near_y = [z], [y]
    for s, h in HOPS[1:]:
        near_z.append(around(z, -d * h if s == "L" else d * h, NZ))
        near_y.append(around(y, -d * h if s == "L" else d * h, NY))
    x_from = (x, around(x, -d, NX), around(x, d, NX), around(x, 2, NX))

    barrier = pltpu.get_barrier_semaphore()
    peers = (*to_z.values(), to_x["L1"], to_x["S1"], to_x["X2"], *to_y.values(), sibling)
    for peer in peers:
        pl.semaphore_signal(barrier, inc=1, device_id=peer, device_id_type=MESH)
    pl.semaphore_wait(barrier, len(peers))

    half = pl.ds(pl.multiple_of(core * HALF, HALF), HALF)

    def body(x0):
        return pl.ds(GROUP * x0, BODY - GROUP * x0)

    tail = pl.ds(BODY, TAIL)

    def v_block(xx, zz):
        return v.at[pl.ds(pl.multiple_of((xx * NZ + zz) * ROWS, ROWS), ROWS)]

    def d_block(xx, zz, columns):
        return dt.at[xx * NZ + zz, half, columns]

    def c_block(yy, j):
        return c.at[j, yy, core] if PIECES == 2 else c.at[:, yy, core]

    def leaving(at, s, h):
        return at[0 if h == 1 else HOPS.index((s, h - 1))]

    def ends(name):
        kind = name[0]
        if kind == "Vz":
            s, h = name[1:]
            block = v_block(x, leaving(near_z, s, h))
            return (v_in if h == 1 else block), block, to_z[s], SENT["V"]
        if kind == "Vx":
            s, k = name[1:]
            if s == "L2" and k in DIRECT:
                s = "X2"
            block = v_block(x_from[1] if s == "L2" else x, near_z[k])
            return (v_in if k == 0 and s != "L2" else block), block, to_x[s], SENT["V"]
        if kind == "Dz":
            x0, s, h = name[1:]
            block = d_block(x0, leaving(near_z, s, h), body(x0))
            return block, block, to_z[s], SENT["D"] + x0
        if kind == "Ds":
            x0 = name[1]
            block = dt.at[pl.ds(x0 * NZ, NZ), half, body(x0)]
            return block, block, sibling, SENT["D"] + x0
        if kind == "Az":
            s, h = name[1:]
            block = d_block(x, leaving(near_z, s, h), tail)
            return (dt_in.at[half, tail] if h == 1 else block), block, to_z[s], SENT["A"]
        if kind == "Ax":
            s = name[1]
            xx = x_from[1] if s == "L2" else x
            block = dt.at[pl.ds(xx * NZ, NZ), half, tail]
            return block, block, to_x[s], SENT["A"]
        if kind == "As":
            block = dt.at[:, half, tail]
            return block, block, sibling, SENT["As"]
        if kind == "Cy":
            s, h, j = name[1:]
            block = c_block(leaving(near_y, s, h), j)
            src = block if h > 1 else (c_in.at[j] if PIECES == 2 else c_in)
            return src, block, to_y[s], SENT["Cy"] + j
        j = name[1]
        block = c.at[j, :, core] if PIECES == 2 else c.at[:, :, core]
        return block, block, sibling, SENT["Cs"] + j

    def arrival(name):
        if name[0] == "Vx" and name[1] in ("S1", "L2"):
            return recv_sem.at[SEM[name[:2]]]
        return recv_sem.at[SEM[name]]

    def start(name):
        src, dst, to, sent = ends(name)
        pltpu.make_async_remote_copy(
            src_ref=src, dst_ref=dst, send_sem=send_sem.at[sent], recv_sem=arrival(name),
            device_id=to, device_id_type=MESH,
        ).start()

    def wait_bytes(ref, sem):
        pltpu.make_async_copy(ref, ref, sem).wait()

    def wait(name):
        if len(name) == 2 and name[0] == "Vx":
            ref = v.at[pl.ds(0, NZ * ROWS)]
        elif name[0] == "Dx":
            ref = d_block(name[1], z, body(name[1]))
        else:
            ref = ends(name)[1]
        wait_bytes(ref, arrival(name))

    def start_own(x0, kind):
        src, dst = dt_in.at[half, body(x0)], d_block(x0, z, body(x0))
        if kind == "x":
            ways = [(to_x[s], SENT["own"], ("Dx", x0)) for s in ("L1", "S1", "X2")]
        else:
            ways = [(to_z[s], SENT["D"] + x0, ("Dz", x0, s, 1)) for s in ("L", "S")]
        for to, sent, name in ways:
            pltpu.make_async_remote_copy(
                src_ref=src, dst_ref=dst, send_sem=send_sem.at[sent], recv_sem=arrival(name),
                device_id=to, device_id_type=MESH,
            ).start()

    def finish_sends():
        wait_bytes(v.at[pl.ds(0, 31 * ROWS)], send_sem.at[SENT["V"]])
        for x0 in range(NX):
            wait_bytes(dt.at[pl.ds(0, 15), pl.ds(0, HALF), body(x0)], send_sem.at[SENT["D"] + x0])
        if TAIL:
            wait_bytes(dt.at[pl.ds(0, 31), pl.ds(0, HALF), tail], send_sem.at[SENT["A"]])
            wait_bytes(dt.at[:, half, tail], send_sem.at[SENT["As"]])
        for j in range(PIECES):
            ring = c.at[j, pl.ds(0, 7), 0] if PIECES == 2 else c.at[:, pl.ds(0, 7), 0]
            wait_bytes(ring, send_sem.at[SENT["Cy"] + j])
            across = c.at[j, :, core] if PIECES == 2 else c.at[:, :, core]
            wait_bytes(across, send_sem.at[SENT["Cs"] + j])
        for x0 in range(NX):
            only_here(
                x0, True,
                lambda x0=x0: wait_bytes(dt.at[pl.ds(0, 3), pl.ds(0, HALF), body(x0)], send_sem.at[SENT["own"]]),
            )

    local = [
        pltpu.make_async_copy(dt_in.at[half], d_block(x, z, pl.ds(0, TILE)), local_sem.at[0]),
        pltpu.make_async_copy(v_in, v_block(x, z), local_sem.at[1]),
    ]
    local += [
        pltpu.make_async_copy(c_in.at[j] if PIECES == 2 else c_in, c_block(y, j), local_sem.at[2 + j])
        for j in range(PIECES)
    ]

    ranks = [
        pltpu.make_async_copy(col_rank_in, col_rank, rank_sem.at[0]),
    ]

    def finish_local():
        for one in local:
            one.wait()

    def only_here(x0, here, make):
        @pl.when(x == x0 if here else x != x0)
        def _():
            make()

    def compute(task):
        kind, b = task
        if kind == "T":
            first = pl.multiple_of(x_from[b] * GROUP, GROUP)
            vt[:, pl.ds(first, GROUP)] = v[pl.ds(first, GROUP)].T
            return
        if kind == "P":
            for a in range(0, GROUP, 256):
                total = None
                for m in range(NX - 1):
                    part = last_columns(m, a)
                    total = part if total is None else total + part
                sa[:, a:a + 256] = total
            return
        lo, hi = GROUP * b, GROUP * (b + 1)
        if kind == "S":
            for a in range(lo, hi, 256):
                e = a + 256
                st[:, a:e] = jnp.dot(
                    vt[:, :e], dt[:e // ROWS, :, a:e].reshape(e, 256), preferred_element_type=F32
                ).astype(BF16)
            return
        for a in range(0, hi, 256):
            e = a + 256
            k = max(lo, a)
            part = lax.dot_general(
                st[:, k:hi], dt[a // ROWS:e // ROWS, :, k:hi].reshape(256, hi - k),
                (((1,), (1,)), ((), ())), preferred_element_type=F32,
            )
            if b < NX - 1:
                na[:, a:e] = part if a >= lo else na[:, a:e] + part
            else:
                nt[:, a:e] = (part if a >= lo else na[:, a:e] + part).astype(BF16)

    def last_columns(m, a):
        first = pl.multiple_of(x_from[m] * GROUP, GROUP)
        columns = dt[pl.ds(x_from[m] * NZ, NZ), :, BODY_ROWS + a:BODY_ROWS + a + 256]
        return jnp.dot(vt[:, pl.ds(first, GROUP)], columns.reshape(GROUP, 256), preferred_element_type=F32)

    def finish():
        for a in range(0, GROUP, 256):
            e = BODY_ROWS + a
            st[:, e:e + 256] = (sa[:, a:a + 256] + last_columns(NX - 1, a)).astype(BF16)
        compute(("N", NX - 1))
        pair = pl.multiple_of((col // 2) * 2 * ROWS, 2 * ROWS)
        both = st[:, pl.ds(pair, 2 * ROWS)].T
        mine = jnp.where(col % 2 == 0, both[:ROWS], both[ROWS:])
        for one in ranks:
            one.wait()
        q = lax.broadcasted_iota(jnp.int32, (ROWS, RANK), 1)
        s_out[...] = jnp.where(q < row_rank[0], mine.astype(F32), 0.0).astype(BF16)
        q = lax.broadcasted_iota(jnp.int32, (RANK, 256), 0)
        p = lax.broadcasted_iota(jnp.int32, (RANK, 256), 1)
        for j in range(2):
            for first in range(0, RANK, 256):
                columns = c[j, :, :, :, first:first + 256].reshape(TILE, 256)
                part = jnp.dot(nt[...], columns, preferred_element_type=F32)
                kept = (q < row_rank[0]) & (p < col_rank[j] - first)
                k_out[j, :, first:first + 256] = jnp.where(kept, part, 0.0).astype(BF16)

    here = False
    for code in ORDER:
        if code in (1000, 1001):
            for x0 in range(NX):
                only_here(x0, True, lambda x0=x0: start_own(x0, "xz"[code - 1000]))
        elif code >= 2000:
            compute(TASKS[code - 2000])
        elif code > 0:
            name = NAMES[code]
            if name[0] == "Dz" and name[3] == 1:
                only_here(name[1], False, lambda name=name: start(name))
            else:
                start(name)
        else:
            if not here:
                for one in local + ranks:
                    one.start()
                finish_local()
                here = True
            name = NAMES[-code]
            if name[0] == "Dx":
                only_here(name[1], False, lambda name=name: wait(name))
            else:
                wait(name)

    finish()
    finish_sends()


VMEM_LIMIT = 48 * 1024 * 1024


def in_hbm(array):
    return pltpu.with_memory_space_constraint(array, pltpu.HBM)


def on_device(diag_inverse, row_v, row_rank, col_v, col_rank):
    vmem = pl.BlockSpec(memory_space=pltpu.VMEM)
    hbm = pl.BlockSpec(memory_space=pltpu.HBM)
    smem = pl.BlockSpec(memory_space=pltpu.SMEM)
    solved, cores = pl.pallas_call(
        kernel,
        out_shape=(
            pltpu.VMEM((ROWS, RANK), BF16),
            pltpu.VMEM((2, RANK, RANK), BF16),
        ),
        in_specs=[hbm, hbm, smem, hbm, hbm],
        out_specs=(vmem, vmem),
        scratch_shapes=[
            pltpu.VMEM((NX * NZ, ROWS, TILE), BF16),
            pltpu.VMEM((TILE, RANK), BF16),
            pltpu.VMEM((2, NY, 2, CROWS, RANK), BF16),
            pltpu.VMEM((RANK, TILE), BF16),
            pltpu.VMEM((RANK, TILE), BF16),
            pltpu.VMEM((RANK, TILE), BF16),
            pltpu.VMEM((RANK, TILE), F32),
            pltpu.VMEM((RANK, GROUP), F32),
            pltpu.SMEM((2,), jnp.int32),
            pltpu.SemaphoreType.DMA((WIDE,)),
            pltpu.SemaphoreType.DMA((len(SEM),)),
            pltpu.SemaphoreType.DMA((4,)),
            pltpu.SemaphoreType.DMA((1,)),
        ],
        compiler_params=pltpu.CompilerParams(
            collective_id=0, has_side_effects=True, vmem_limit_bytes=VMEM_LIMIT
        ),
    )(in_hbm(diag_inverse.T), in_hbm(row_v[0]), row_rank, in_hbm(col_v), in_hbm(col_rank))
    return solved[None], cores[None]


def solution(mesh):
    in_specs = (P(None, "col"), P("row", "col", None), P("row"), P("col", "row", None), P("col"))
    out_specs = (P("row", "col", None), P("row", "col", None, None))
    return jax.shard_map(
        on_device, mesh=mesh, in_specs=in_specs, out_specs=out_specs, check_vma=False
    )
```

```python
import jax
import jax.numpy as jnp
from jax import lax
from jax.experimental import pallas as pl
from jax.experimental.pallas import tpu as pltpu
from jax.sharding import PartitionSpec as P

MESH = pl.DeviceIdType.MESH
BF16 = jnp.bfloat16
F32 = jnp.float32
TILE = 2048
RANK = 512
NX, NY, NZ = 4, 8, 8
ROWS = TILE // (NX * NZ)
HALF = ROWS // 2
GROUP = TILE // NX
CROWS = TILE // (2 * NY)
TAIL = 384
BODY = TILE - TAIL
BODY_ROWS = TILE - GROUP
PIECES = 2
DIRECT = (0, 7,)
HOPS = ((), ("L", 1), ("S", 1), ("L", 2), ("S", 2), ("L", 3), ("S", 3), ("L", 4))
WAYS = (("L", 4), ("S", 3))

ORDER = (
    1000, 1, 24, 87, 68, 79, 16, 88, 5, 80, 1001, 72, -35, 61, 57, -1, 2, 9, -34, 50, -5, 6, 10, 8, -68, 54, -33,
    69, 43, 25, -32, 36, -57, 26, -87, 89, 58, -72, -79, 40, 81, 47, -2, 3, 73, 11, -6, 28, -69, -80, 82, 12, 7,
    -50, 51, -9, -61, 62, -10, -43, -88, 90, 18, 27, 70, -36, 17, 44, 37, -47, -58, -11, 19, -3, 4, -40, -89, -81,
    83, -54, 29, 59, 13, -73, -51, 48, -62, -12, 41, 20, -70, 74, -82, 84, -7, -90, 92, 71, 30, -44, 14, 45, 63, 91,
    55, -37, 52, -4, 31, 38, -59, 23, 15, -13, -41, -48, -83, 85, 42, -71, -74, 75, 49, 21, -55, -45, -14, 46, -8,
    -38, 39, -84, 86, 22, -15, -52, 53, -63, -92, -95, 2000, 77, 56, -42, 60, -91, 2002, -49, -85, 93, -46, 65, -75,
    76, 1003, -39, 64, -93, -53, 2001, -56, -65, -60, 67, -96, 2003, 66, -86, 94, -64, 2004, 2005, 2006, -66, -77,
    2008, -76, 78, 2007, -67, -94, 2009, -78, 2010,
)
TASKS = tuple(("T", m) for m in range(NX)) + tuple((s, b) for b in range(NX - 1) for s in ("S", "N")) + (("P", 3),)


def copy_names():
    out = [("Vz", s, h) for s, n in WAYS for h in range(1, n + 1)]
    out += [("Vx", s, k) for s in ("L1", "L2", "S1") for k in range(NZ)]
    out += [("Dx", x0) for x0 in range(NX)]
    out += [("Dz", x0, s, h) for x0 in range(NX) for s, n in WAYS for h in range(1, n + 1)]
    out += [("Ds", x0) for x0 in range(NX)]
    out += [("Az", s, h) for s, n in WAYS for h in range(1, n + 1)]
    out += [("Ax", s) for s in ("L1", "L2", "S1")] + [("As", 0)]
    out += [("Cy", s, h, j) for s, n in WAYS for h in range(1, n + 1) for j in range(PIECES)]
    out += [("Cs", j) for j in range(PIECES)]
    out += [("Vx", "S1"), ("Vx", "L2")]
    return out


NAMES = [None] + copy_names()
SEM = {n: i - 1 for i, n in enumerate(NAMES) if i}
SENT = {"V": 0, "A": 1, "As": 2, "own": 3, "D": 4, "Cy": 8, "Cs": 10}
WIDE = 12


def kernel(
    dt_in, v_in, row_rank, c_in, col_rank_in, s_out, k_out, dt, v, c, vt, st, nt, na, sa, col_rank,
    send_sem, recv_sem, local_sem, rank_sem,
):
    row = lax.axis_index("row")
    col = lax.axis_index("col")
    core = lax.rem(row, 2)
    y = lax.div(row, 2)
    x = lax.div(col, NZ)
    z = lax.rem(col, NZ)
    d = 1 - 2 * core

    def around(at, step, n):
        return lax.rem(at + step + n, n)

    def at_z(step):
        return row, x * NZ + around(z, step, NZ)

    def at_x(step):
        return row, around(x, step, NX) * NZ + z

    def at_y(step):
        return around(y, step, NY) * 2 + core, col

    sibling = (y * 2 + 1 - core, col)
    to_z = {"L": at_z(d), "S": at_z(-d)}
    to_y = {"L": at_y(d), "S": at_y(-d)}
    to_x = {"L1": at_x(d), "L2": at_x(d), "S1": at_x(-d), "X2": at_x(2)}
    near_z, near_y = [z], [y]
    for s, h in HOPS[1:]:
        near_z.append(around(z, -d * h if s == "L" else d * h, NZ))
        near_y.append(around(y, -d * h if s == "L" else d * h, NY))
    x_from = (x, around(x, -d, NX), around(x, d, NX), around(x, 2, NX))

    barrier = pltpu.get_barrier_semaphore()
    peers = (*to_z.values(), to_x["L1"], to_x["S1"], to_x["X2"], *to_y.values(), sibling)
    for peer in peers:
        pl.semaphore_signal(barrier, inc=1, device_id=peer, device_id_type=MESH)
    pl.semaphore_wait(barrier, len(peers))

    half = pl.ds(pl.multiple_of(core * HALF, HALF), HALF)

    def body(x0):
        return pl.ds(GROUP * x0, BODY - GROUP * x0)

    tail = pl.ds(BODY, TAIL)

    def v_block(xx, zz):
        return v.at[pl.ds(pl.multiple_of((xx * NZ + zz) * ROWS, ROWS), ROWS)]

    def d_block(xx, zz, columns):
        return dt.at[xx * NZ + zz, half, columns]

    def c_block(yy, j):
        return c.at[j, yy, core] if PIECES == 2 else c.at[:, yy, core]

    def leaving(at, s, h):
        return at[0 if h == 1 else HOPS.index((s, h - 1))]

    def ends(name):
        kind = name[0]
        if kind == "Vz":
            s, h = name[1:]
            block = v_block(x, leaving(near_z, s, h))
            return (v_in if h == 1 else block), block, to_z[s], SENT["V"]
        if kind == "Vx":
            s, k = name[1:]
            if s == "L2" and k in DIRECT:
                s = "X2"
            block = v_block(x_from[1] if s == "L2" else x, near_z[k])
            return (v_in if k == 0 and s != "L2" else block), block, to_x[s], SENT["V"]
        if kind == "Dz":
            x0, s, h = name[1:]
            block = d_block(x0, leaving(near_z, s, h), body(x0))
            return block, block, to_z[s], SENT["D"] + x0
        if kind == "Ds":
            x0 = name[1]
            block = dt.at[pl.ds(x0 * NZ, NZ), half, body(x0)]
            return block, block, sibling, SENT["D"] + x0
        if kind == "Az":
            s, h = name[1:]
            block = d_block(x, leaving(near_z, s, h), tail)
            return (dt_in.at[half, tail] if h == 1 else block), block, to_z[s], SENT["A"]
        if kind == "Ax":
            s = name[1]
            xx = x_from[1] if s == "L2" else x
            block = dt.at[pl.ds(xx * NZ, NZ), half, tail]
            return block, block, to_x[s], SENT["A"]
        if kind == "As":
            block = dt.at[:, half, tail]
            return block, block, sibling, SENT["As"]
        if kind == "Cy":
            s, h, j = name[1:]
            block = c_block(leaving(near_y, s, h), j)
            src = block if h > 1 else (c_in.at[j] if PIECES == 2 else c_in)
            return src, block, to_y[s], SENT["Cy"] + j
        j = name[1]
        block = c.at[j, :, core] if PIECES == 2 else c.at[:, :, core]
        return block, block, sibling, SENT["Cs"] + j

    def arrival(name):
        if name[0] == "Vx" and name[1] in ("S1", "L2"):
            return recv_sem.at[SEM[name[:2]]]
        return recv_sem.at[SEM[name]]

    def start(name):
        src, dst, to, sent = ends(name)
        pltpu.make_async_remote_copy(
            src_ref=src, dst_ref=dst, send_sem=send_sem.at[sent], recv_sem=arrival(name),
            device_id=to, device_id_type=MESH,
        ).start()

    def wait_bytes(ref, sem):
        pltpu.make_async_copy(ref, ref, sem).wait()

    def wait(name):
        if len(name) == 2 and name[0] == "Vx":
            ref = v.at[pl.ds(0, NZ * ROWS)]
        elif name[0] == "Dx":
            ref = d_block(name[1], z, body(name[1]))
        else:
            ref = ends(name)[1]
        wait_bytes(ref, arrival(name))

    def start_own(x0, kind):
        src, dst = dt_in.at[half, body(x0)], d_block(x0, z, body(x0))
        if kind == "x":
            ways = [(to_x[s], SENT["own"], ("Dx", x0)) for s in ("L1", "S1", "X2")]
        else:
            ways = [(to_z[s], SENT["D"] + x0, ("Dz", x0, s, 1)) for s in ("L", "S")]
        for to, sent, name in ways:
            pltpu.make_async_remote_copy(
                src_ref=src, dst_ref=dst, send_sem=send_sem.at[sent], recv_sem=arrival(name),
                device_id=to, device_id_type=MESH,
            ).start()

    def finish_sends():
        wait_bytes(v.at[pl.ds(0, 31 * ROWS)], send_sem.at[SENT["V"]])
        for x0 in range(NX):
            wait_bytes(dt.at[pl.ds(0, 15), pl.ds(0, HALF), body(x0)], send_sem.at[SENT["D"] + x0])
        if TAIL:
            wait_bytes(dt.at[pl.ds(0, 31), pl.ds(0, HALF), tail], send_sem.at[SENT["A"]])
            wait_bytes(dt.at[:, half, tail], send_sem.at[SENT["As"]])
        for j in range(PIECES):
            ring = c.at[j, pl.ds(0, 7), 0] if PIECES == 2 else c.at[:, pl.ds(0, 7), 0]
            wait_bytes(ring, send_sem.at[SENT["Cy"] + j])
            across = c.at[j, :, core] if PIECES == 2 else c.at[:, :, core]
            wait_bytes(across, send_sem.at[SENT["Cs"] + j])
        for x0 in range(NX):
            only_here(
                x0, True,
                lambda x0=x0: wait_bytes(dt.at[pl.ds(0, 3), pl.ds(0, HALF), body(x0)], send_sem.at[SENT["own"]]),
            )

    local = [
        pltpu.make_async_copy(dt_in.at[half], d_block(x, z, pl.ds(0, TILE)), local_sem.at[0]),
        pltpu.make_async_copy(v_in, v_block(x, z), local_sem.at[1]),
    ]
    local += [
        pltpu.make_async_copy(c_in.at[j] if PIECES == 2 else c_in, c_block(y, j), local_sem.at[2 + j])
        for j in range(PIECES)
    ]

    ranks = [
        pltpu.make_async_copy(col_rank_in, col_rank, rank_sem.at[0]),
    ]

    def finish_local():
        for one in local:
            one.wait()

    def only_here(x0, here, make):
        @pl.when(x == x0 if here else x != x0)
        def _():
            make()

    def compute(task):
        kind, b = task
        if kind == "T":
            first = pl.multiple_of(x_from[b] * GROUP, GROUP)
            vt[:, pl.ds(first, GROUP)] = v[pl.ds(first, GROUP)].T
            return
        if kind == "P":
            for a in range(0, GROUP, 256):
                total = None
                for m in range(NX - 1):
                    part = last_columns(m, a)
                    total = part if total is None else total + part
                sa[:, a:a + 256] = total
            return
        lo, hi = GROUP * b, GROUP * (b + 1)
        if kind == "S":
            for a in range(lo, hi, 256):
                e = a + 256
                st[:, a:e] = jnp.dot(
                    vt[:, :e], dt[:e // ROWS, :, a:e].reshape(e, 256), preferred_element_type=F32
                ).astype(BF16)
            return
        for a in range(0, hi, 256):
            e = a + 256
            k = max(lo, a)
            part = lax.dot_general(
                st[:, k:hi], dt[a // ROWS:e // ROWS, :, k:hi].reshape(256, hi - k),
                (((1,), (1,)), ((), ())), preferred_element_type=F32,
            )
            if b < NX - 1:
                na[:, a:e] = part if a >= lo else na[:, a:e] + part
            else:
                nt[:, a:e] = (part if a >= lo else na[:, a:e] + part).astype(BF16)

    def last_columns(m, a):
        first = pl.multiple_of(x_from[m] * GROUP, GROUP)
        columns = dt[pl.ds(x_from[m] * NZ, NZ), :, BODY_ROWS + a:BODY_ROWS + a + 256]
        return jnp.dot(vt[:, pl.ds(first, GROUP)], columns.reshape(GROUP, 256), preferred_element_type=F32)

    def finish():
        for a in range(0, GROUP, 256):
            e = BODY_ROWS + a
            st[:, e:e + 256] = (sa[:, a:a + 256] + last_columns(NX - 1, a)).astype(BF16)
        compute(("N", NX - 1))
        pair = pl.multiple_of((col // 2) * 2 * ROWS, 2 * ROWS)
        both = st[:, pl.ds(pair, 2 * ROWS)].T
        mine = jnp.where(col % 2 == 0, both[:ROWS], both[ROWS:])
        for one in ranks:
            one.wait()
        q = lax.broadcasted_iota(jnp.int32, (ROWS, RANK), 1)
        s_out[...] = jnp.where(q < row_rank[0], mine.astype(F32), 0.0).astype(BF16)
        q = lax.broadcasted_iota(jnp.int32, (RANK, 256), 0)
        p = lax.broadcasted_iota(jnp.int32, (RANK, 256), 1)
        for j in range(2):
            for first in range(0, RANK, 256):
                columns = c[j, :, :, :, first:first + 256].reshape(TILE, 256)
                part = jnp.dot(nt[...], columns, preferred_element_type=F32)
                kept = (q < row_rank[0]) & (p < col_rank[j] - first)
                k_out[j, :, first:first + 256] = jnp.where(kept, part, 0.0).astype(BF16)

    here = False
    passed = False
    for position, code in enumerate(ORDER):
        if code in (1000, 1001):
            for x0 in range(NX):
                only_here(x0, True, lambda x0=x0: start_own(x0, "xz"[code - 1000]))
        elif code == 1003:
            late = [b for b in ORDER[:position] if b >= 2000]

            @pl.when(z > EARLY)
            def _():
                for b in late:
                    compute(TASKS[b - 2000])

            passed = True
        elif code >= 2000 and passed:
            compute(TASKS[code - 2000])
        elif code >= 2000:
            pl.when(z <= EARLY)(lambda code=code: compute(TASKS[code - 2000]))
        elif code > 0:
            name = NAMES[code]
            if name[0] == "Dz" and name[3] == 1:
                only_here(name[1], False, lambda name=name: start(name))
            else:
                start(name)
        else:
            if not here:
                for one in local + ranks:
                    one.start()
                finish_local()
                here = True
            name = NAMES[-code]
            if name[0] == "Dx":
                only_here(name[1], False, lambda name=name: wait(name))
            else:
                wait(name)

    finish()
    finish_sends()


EARLY = 1
VMEM_LIMIT = 48 * 1024 * 1024


def in_hbm(array):
    return pltpu.with_memory_space_constraint(array, pltpu.HBM)


def on_device(diag_inverse, row_v, row_rank, col_v, col_rank):
    vmem = pl.BlockSpec(memory_space=pltpu.VMEM)
    hbm = pl.BlockSpec(memory_space=pltpu.HBM)
    smem = pl.BlockSpec(memory_space=pltpu.SMEM)
    solved, cores = pl.pallas_call(
        kernel,
        out_shape=(
            pltpu.VMEM((ROWS, RANK), BF16),
            pltpu.VMEM((2, RANK, RANK), BF16),
        ),
        in_specs=[hbm, hbm, smem, hbm, hbm],
        out_specs=(vmem, vmem),
        scratch_shapes=[
            pltpu.VMEM((NX * NZ, ROWS, TILE), BF16),
            pltpu.VMEM((TILE, RANK), BF16),
            pltpu.VMEM((2, NY, 2, CROWS, RANK), BF16),
            pltpu.VMEM((RANK, TILE), BF16),
            pltpu.VMEM((RANK, TILE), BF16),
            pltpu.VMEM((RANK, TILE), BF16),
            pltpu.VMEM((RANK, TILE), F32),
            pltpu.VMEM((RANK, GROUP), F32),
            pltpu.SMEM((2,), jnp.int32),
            pltpu.SemaphoreType.DMA((WIDE,)),
            pltpu.SemaphoreType.DMA((len(SEM),)),
            pltpu.SemaphoreType.DMA((4,)),
            pltpu.SemaphoreType.DMA((1,)),
        ],
        compiler_params=pltpu.CompilerParams(
            collective_id=0, has_side_effects=True, vmem_limit_bytes=VMEM_LIMIT
        ),
    )(in_hbm(diag_inverse.T), in_hbm(row_v[0]), row_rank, in_hbm(col_v), in_hbm(col_rank))
    return solved[None], cores[None]


def solution(mesh):
    in_specs = (P(None, "col"), P("row", "col", None), P("row"), P("col", "row", None), P("col"))
    out_specs = (P("row", "col", None), P("row", "col", None, None))
    return jax.shard_map(
        on_device, mesh=mesh, in_specs=in_specs, out_specs=out_specs, check_vma=False
    )
```
